32 devices in a mesh: groups: 2 (over y), row: 16 (over z, x, core).
Axes of the slice: x: 2, y: 2, z: 4, core: 2. Of those that a mesh axis runs over, the one named last changes fastest.
Arguments:
- activations: bfloat16 [768, 8192], P('groups', 'row'), parts along dimension 0, may hold values from -24 to 24
- norm_gain: bfloat16 [8192], P('row'), may hold values from 0.099609375 to 1.8984375
- gate_weight: bfloat16 [8192, 28672], P(None, 'row'), may hold values from -0.0625 to 0.0625
- up_weight: bfloat16 [8192, 28672], P(None, 'row'), may hold values from -0.0625 to 0.0625
- down_weight: bfloat16 [28672, 8192], P('row'), may hold values from -0.046875 to 0.046875
Outputs:
- mlp_out: bfloat16 [768, 8192], P('groups', 'row'), parts along dimension 0
The draws below stay inside these ranges and needn't reach their ends.
There are 2 independent parts, one for each index of `groups`. The reference program is written for one: setup_inputs(seed, part) draws one part's arguments, and reference() takes and returns one part's arrays. A program takes and returns all parts, laid end to end along the dimension named above; an argument that names none is the same for every part. Nothing has to cross between parts.
All inputs are finite; a program needn't handle non-finite values.
Results may differ from the reference program's by a relative error of at most 0.0065.
Values may be sent and summed in bfloat16 or wider, within the bound.
No kernel may reach another device: no remote copies, remote signals or barrier semaphores. Data moves between devices by JAX's collectives and lax.ppermute only.
A program may use at most 192 MiB of HBM per device.

```python
import jax
import jax.numpy as jnp
from jax import lax

D = 8192
FF = 28672
TOKENS = 384


def draw_activations(key, part):
    key_cols, key_rows, key_base = jax.random.split(key, 3)
    position = jnp.arange(D, dtype=jnp.float32) / max(D - 1, 1)
    column_scale = jnp.exp(jax.random.uniform(key_cols, (D,), jnp.float32) * jnp.log(10.0))
    row_scale = jnp.exp(jax.random.uniform(key_rows, (TOKENS, 1), jnp.float32) * jnp.log(10.0))
    rising = 3.0 ** position
    base_values = jax.random.truncated_normal(key_base, -4.0, 4.0, (TOKENS, D), jnp.float32)
    result = jnp.clip(base_values * row_scale * (column_scale * rising)[None, :] * 0.05, -24.0, 24.0)
    return result.astype(jnp.bfloat16)


def strengthened(values, rng, source, target, shards_of, factor):
    owner, partner = [(jnp.arange(values.shape[dim]) // (values.shape[dim] // shards_of)).reshape([-1 if axis == dim else 1 for axis in range(values.ndim)]) for dim in (source, target)]
    chosen = jax.random.permutation(rng, shards_of)[partner]
    strong = (owner == chosen) | (owner == (partner + shards_of // 2) % shards_of)
    return jnp.where(strong, factor * values, values)


def block_scale(rng, shape, pieces, low, top_value):
    def one(dim, parts):
        heights = jax.random.uniform(jax.random.fold_in(jax.random.fold_in(rng, 6), dim), (parts,), jnp.float32, low / len(pieces), top_value / len(pieces))
        return jnp.repeat(jnp.exp(heights), shape[dim] // parts).reshape((-1,) + (1,) * (len(shape) - dim - 1))

    gain = one(*pieces[0])
    for cut in pieces[1:]:
        gain = gain * one(*cut)
    return gain


def bell_draw(key, extent, spread, limit, shards=(), kind=jnp.bfloat16):
    values = jax.random.normal(key, extent, jnp.float32) * spread
    if len(shards) > 0:
        values = block_scale(key, extent, shards, -0.22, 0.18) * values
    return jnp.clip(values, min=-limit, max=limit).astype(kind)


def gaussian_with(own_key, extent, scale, reach, cuts, heavy, held_as=jnp.bfloat16):
    values = scale * jax.random.normal(own_key, extent, jnp.float32)
    if cuts:
        values = values * block_scale(own_key, extent, cuts, -0.22, 0.18)
    return jnp.clip(strengthened(values, jax.random.fold_in(own_key, 3), *heavy), -reach, reach).astype(held_as)


def setup_inputs(seed: int = 0, part: int = 0) -> dict:
    arg_keys = jax.random.split(jax.random.key(seed), 6)
    own_keys = jax.random.split(jax.random.fold_in(arg_keys[5], part), 6)
    activations = draw_activations(jax.random.fold_in(jax.random.fold_in(arg_keys[5], part), 71), part)
    norm_gain = jnp.clip(1.0 + 0.18 * jax.random.normal(arg_keys[1], (D,), jnp.float32), 0.099609375, 1.8984375).astype(jnp.bfloat16)
    gate_weight = bell_draw(arg_keys[2], (D, FF), D ** -0.5, 0.0625, ((1, 16),))
    up_weight = bell_draw(arg_keys[3], (D, FF), D ** -0.5, 0.0625, ((1, 16),))
    down_weight = gaussian_with(arg_keys[4], (FF, D), FF ** -0.5, 0.046875, ((0, 16),), (0, 1, 16, 2.0))
    return {"activations": activations, "norm_gain": norm_gain, "gate_weight": gate_weight, "up_weight": up_weight, "down_weight": down_weight}


def reference(activations, norm_gain, gate_weight, up_weight, down_weight):
    float_rows = activations.astype(jnp.float32)
    mean_square = lax.optimization_barrier(jnp.mean(float_rows * float_rows, axis=1, keepdims=True))
    normed = (float_rows * lax.rsqrt(mean_square + 1e-05) * norm_gain.astype(jnp.float32)[None, :]).astype(jnp.bfloat16)
    gate_proj = jnp.dot(normed, gate_weight, preferred_element_type=jnp.float32)
    up_proj = jnp.dot(normed, up_weight, preferred_element_type=jnp.float32)
    hidden = (jax.nn.silu(gate_proj) * up_proj).astype(jnp.bfloat16)
    return jnp.dot(hidden, down_weight, preferred_element_type=jnp.float32).astype(jnp.bfloat16)
```

```python
import functools

import jax
import jax.numpy as jnp
from jax import lax
from jax.experimental import pallas as pl
from jax.experimental.pallas import tpu as pltpu
from jax.sharding import PartitionSpec as P

EPS = 1e-05
AXIS = "row"
VMEM_LIMIT = 40 * 1024 * 1024


def plain_per_device(features, activations, norm_gain, gate_weight, up_weight, down_weight):
    float_rows = activations.astype(jnp.float32)
    square_sums = lax.psum(jnp.sum(float_rows * float_rows, axis=1), AXIS)
    inv_scale = lax.rsqrt(square_sums / features + EPS)
    normed = (float_rows * inv_scale[:, None] * norm_gain.astype(jnp.float32)[None, :]).astype(
        jnp.bfloat16
    )
    shard_rows = lax.all_gather(normed, AXIS, axis=1, tiled=True)
    gate_proj = jnp.dot(shard_rows, gate_weight, preferred_element_type=jnp.float32)
    up_proj = jnp.dot(shard_rows, up_weight, preferred_element_type=jnp.float32)
    hidden = (jax.nn.silu(gate_proj) * up_proj).astype(jnp.bfloat16)
    reduced = lax.psum_scatter(
        lax.dot_general(
            down_weight, hidden, (((0,), (1,)), ((), ())), preferred_element_type=jnp.float32
        ),
        AXIS,
        scatter_dimension=0,
        tiled=True,
    )
    return reduced.T.astype(jnp.bfloat16)


def swap(value, mask):
    return lax.ppermute(value, AXIS, [(i, i ^ mask) for i in range(lax.axis_size(AXIS))])


def gate_up_kernel(pairs, first, last, place, inv_ref, gain_ref, *refs):
    chunks, refs = refs[: 2 * pairs], refs[2 * pairs :]
    gate_w, up_w, refs = refs[0], refs[1], refs[2:]
    if not first:
        gate_in, up_in, refs = refs[0], refs[1], refs[2:]
    if last:
        hidden_ref, gate_out, up_out, normed = refs
    else:
        gate_out, up_out, normed = refs
    step, half = pl.program_id(0), pl.program_id(1)
    width = chunks[0].shape[1]
    cols = gate_w.shape[1]
    core = place[pairs]

    for k in range(pairs):

        @pl.when((step == k) & (half == 0))
        def _(k=k):
            inv = inv_ref[:, :1]
            for which, ref in enumerate(chunks[2 * k : 2 * k + 2]):
                start = pl.multiple_of((core ^ which) * width, width)
                scaled = ref[...].astype(jnp.float32) * inv * gain_ref[k : k + 1, pl.ds(start, width)]
                normed[:, pl.ds(start, width)] = scaled.astype(jnp.bfloat16)

    where = pl.ds(pl.multiple_of(half * cols, cols), cols)
    for w_ref, src, out in (
        (gate_w, None if first else gate_in, gate_out),
        (up_w, None if first else up_in, up_out),
    ):
        product = jnp.dot(normed[...], w_ref[...], preferred_element_type=jnp.float32)

        @pl.when(step == 0)
        def _(product=product, src=src, out=out):
            if src is None:
                out[:, where] = product
            else:
                out[:, where] = src[:, where] + product

        @pl.when(step != 0)
        def _(product=product, out=out):
            out[:, where] += product

    if last:

        @pl.when(step == pairs - 1)
        def _():
            gate = gate_out[:, where]
            value = gate / (1.0 + jnp.exp(-gate)) * up_out[:, where]
            hidden_ref[:, where] = value.astype(jnp.bfloat16)


def gate_up(place, inv, gains, chunks, gate_weight, up_weight, sums, last):
    pairs = len(chunks) // 2
    tokens, width = chunks[0].shape
    units = gate_weight.shape[1]
    halves = 2
    cols = units // halves
    whole = lambda: pl.BlockSpec(memory_space=pltpu.VMEM)
    weight = lambda: pl.BlockSpec((2 * width, cols), lambda s, h, place: (place[s], h))
    first = sums is None
    acc = jax.ShapeDtypeStruct((tokens, units), jnp.float32)
    out_shape = [] if last else [acc, acc]
    scratch = [pltpu.VMEM((tokens, 2 * width), jnp.bfloat16)]
    aliases = {}
    operands = [place, inv, gains, *chunks, gate_weight, up_weight]
    in_specs = [whole() for _ in range(2 + len(chunks))] + [weight(), weight()]
    if not first:
        if not last:
            aliases = {len(operands): 0, len(operands) + 1: 1}
        operands += list(sums)
        in_specs += [whole(), whole()]
    if last:
        out_shape = [jax.ShapeDtypeStruct((tokens, units), jnp.bfloat16)]
        scratch = [pltpu.VMEM((tokens, units), jnp.float32)] * 2 + scratch
    return pl.pallas_call(
        functools.partial(gate_up_kernel, pairs, first, last),
        grid_spec=pltpu.PrefetchScalarGridSpec(
            num_scalar_prefetch=1,
            grid=(pairs, halves),
            in_specs=in_specs,
            out_specs=[whole() for _ in out_shape],
            scratch_shapes=scratch,
        ),
        out_shape=out_shape,
        input_output_aliases=aliases,
        compiler_params=pltpu.CompilerParams(vmem_limit_bytes=VMEM_LIMIT),
        cost_estimate=pl.CostEstimate(
            flops=2 * tokens * 2 * width * pairs * units * 2,
            bytes_accessed=2 * 2 * width * pairs * units * 2,
            transcendentals=0,
        ),
        name="gate_up",
    )(*operands)


def down_kernel(place, hidden_ref, w_ref, send_ref, keep_ref):
    product = jnp.dot(hidden_ref[...], w_ref[...], preferred_element_type=jnp.float32)
    step = pl.program_id(0)

    @pl.when(step % 2 == 0)
    def _():
        send_ref[0] = product.astype(jnp.bfloat16)

    @pl.when(step % 2 == 1)
    def _():
        keep_ref[0] = product


def down(place, hidden, down_weight, width):
    tokens, units = hidden.shape
    blocks = place.shape[0]
    return pl.pallas_call(
        down_kernel,
        grid_spec=pltpu.PrefetchScalarGridSpec(
            num_scalar_prefetch=1,
            grid=(blocks,),
            in_specs=[
                pl.BlockSpec(memory_space=pltpu.VMEM),
                pl.BlockSpec((units, width), lambda s, place: (0, place[s])),
            ],
            out_specs=[
                pl.BlockSpec((1, tokens, width), lambda s, place: (s // 2, 0, 0)),
                pl.BlockSpec((1, tokens, width), lambda s, place: (s // 2, 0, 0)),
            ],
        ),
        out_shape=[
            jax.ShapeDtypeStruct((blocks // 2, tokens, width), jnp.bfloat16),
            jax.ShapeDtypeStruct((blocks // 2, tokens, width), jnp.float32),
        ],
        compiler_params=pltpu.CompilerParams(vmem_limit_bytes=VMEM_LIMIT),
        cost_estimate=pl.CostEstimate(
            flops=2 * tokens * units * width * blocks,
            bytes_accessed=2 * units * width * blocks,
            transcendentals=0,
        ),
        name="down",
    )(place, hidden, down_weight)


CORE, X, Z1, Z2, Z3 = 1, 2, 4, 8, 12


def per_device(activations, norm_gain, gate_weight, up_weight, down_weight):
    tokens, width = activations.shape
    features = gate_weight.shape[0]
    me = lax.axis_index(AXIS)
    chip, core = me // 2, me % 2
    is_odd = core == 1

    own = activations
    raw = {0: own}
    raw[Z1] = swap(own, Z1)
    raw[Z3] = swap(own, Z3)
    raw[X] = swap(own, X)
    raw[Z1 | X] = swap(raw[Z1], X)
    raw[Z2] = swap(raw[Z3], Z1)
    raw[Z3 | X] = swap(raw[Z3], X)
    raw[Z2 | X] = swap(raw[Z2], X)
    for mask in (0, X, Z1, Z1 | X, Z3, Z3 | X, Z2, Z2 | X):
        raw[mask | CORE] = swap(raw[mask], CORE)

    rows = own.astype(jnp.float32)
    sums = jnp.sum(rows * rows, axis=1)
    gains = norm_gain.astype(jnp.float32)
    got = swap(jnp.concatenate([sums, gains]), CORE)
    sums = sums + got[:tokens]
    other = got[tokens:]
    gains = jnp.where(is_odd, jnp.concatenate([other, gains]), jnp.concatenate([gains, other]))
    got = swap(jnp.concatenate([sums, gains]), X)
    sums = sums + got[:tokens]
    gains = jnp.concatenate([gains, got[tokens:]])
    message = jnp.concatenate([sums, gains])
    got = {mask: swap(message, mask) for mask in (Z1, Z2, Z3)}
    sums = sums + got[Z1][:tokens] + got[Z2][:tokens] + got[Z3][:tokens]
    gain_of = {0: gains, **{mask: got[mask][tokens:] for mask in got}}
    gain_of = {m: g.reshape(2, 2 * width) for m, g in gain_of.items()}
    inv = lax.rsqrt(sums / features + EPS)
    inv = jnp.broadcast_to(inv[:, None], (tokens, 128))

    acc = None
    stages = [(0, (0, X)), (Z1, (0, X)), (Z3, (0, X)), (Z2, (0,)), (Z2, (X,))]
    for n, (plane, sides) in enumerate(stages):
        masks = [plane | side for side in sides]
        place = jnp.stack([chip ^ (m // 2) for m in masks] + [core]).astype(jnp.int32)
        gain = gain_of[plane]
        if len(sides) == 1:
            gain = gain[sides[0] // X][None]
        chunks = [raw[m | c] for m in masks for c in (0, CORE)]
        acc = gate_up(
            place, inv, gain, chunks, gate_weight, up_weight, acc, n == len(stages) - 1
        )
    hidden = acc[0]

    def plane_sum(plane):
        place = jnp.stack([me ^ (plane | m) for m in (X | CORE, X, CORE, 0)]).astype(jnp.int32)
        send, keep = down(place, hidden, down_weight, width)
        pair = keep + swap(send, CORE).astype(jnp.float32)
        there = swap(pair[0].astype(jnp.bfloat16), X)
        return pair[1] + there.astype(jnp.float32)

    far = swap(plane_sum(Z2).astype(jnp.bfloat16), Z1).astype(jnp.float32)
    far = swap((plane_sum(Z3) + far).astype(jnp.bfloat16), Z3).astype(jnp.float32)
    near = swap(plane_sum(Z1).astype(jnp.bfloat16), Z1).astype(jnp.float32)
    return (plane_sum(0) + near + far).astype(jnp.bfloat16)


def solution(mesh):
    in_specs = (P("groups", AXIS), P(AXIS), P(None, AXIS), P(None, AXIS), P(AXIS, None))
    out_specs = P("groups", AXIS)

    def body(activations, norm_gain, gate_weight, up_weight, down_weight):
        if mesh.shape[AXIS] == 16 and activations.shape[1] % 128 == 0:
            run = per_device
        else:
            run = functools.partial(plain_per_device, gate_weight.shape[0])
        return run(activations, norm_gain, gate_weight, up_weight, down_weight)

    return jax.shard_map(
        body, mesh=mesh, in_specs=in_specs, out_specs=out_specs, check_vma=False
    )
```

```python
import functools

import jax
import jax.numpy as jnp
from jax import lax
from jax.experimental import pallas as pl
from jax.experimental.pallas import tpu as pltpu
from jax.sharding import PartitionSpec as P

EPS = 1e-05
AXIS = "row"
VMEM_LIMIT = 16 * 1024 * 1024


def plain_per_device(features, activations, norm_gain, gate_weight, up_weight, down_weight):
    float_rows = activations.astype(jnp.float32)
    square_sums = lax.psum(jnp.sum(float_rows * float_rows, axis=1), AXIS)
    inv_scale = lax.rsqrt(square_sums / features + EPS)
    normed = (float_rows * inv_scale[:, None] * norm_gain.astype(jnp.float32)[None, :]).astype(
        jnp.bfloat16
    )
    shard_rows = lax.all_gather(normed, AXIS, axis=1, tiled=True)
    gate_proj = jnp.dot(shard_rows, gate_weight, preferred_element_type=jnp.float32)
    up_proj = jnp.dot(shard_rows, up_weight, preferred_element_type=jnp.float32)
    hidden = (jax.nn.silu(gate_proj) * up_proj).astype(jnp.bfloat16)
    reduced = lax.psum_scatter(
        lax.dot_general(
            down_weight, hidden, (((0,), (1,)), ((), ())), preferred_element_type=jnp.float32
        ),
        AXIS,
        scatter_dimension=0,
        tiled=True,
    )
    return reduced.T.astype(jnp.bfloat16)


def swap(value, mask):
    return lax.ppermute(value, AXIS, [(i, i ^ mask) for i in range(lax.axis_size(AXIS))])


COLS = 256
EXTRA = 16
GATE_UP_SHARE, DOWN_SHARE = (1, 1, 1, 1, 1, 1, 1, 1), 1


def cost(flops, weight_bytes, share):
    return pl.CostEstimate(
        flops=int(flops * share), bytes_accessed=int(weight_bytes * share), transcendentals=0
    )


def fetch(copies):
    for copy in copies:
        copy.start()


def landed(copies):
    for copy in copies:
        copy.wait()


def chip_of(mask):
    return lax.axis_index(AXIS) // 2 ^ mask // 2


def gate_up_fetch(block, gate_hbm, up_hbm, into, sems, cols=slice(None)):
    depth = into.shape[1]
    rows = pl.ds(pl.multiple_of(block * depth, depth), depth)
    return [
        pltpu.make_async_copy(hbm.at[rows, cols], into.at[n, :, cols], sems.at[n])
        for n, hbm in enumerate((gate_hbm, up_hbm))
    ]


def down_fetch(block, down_hbm, into, sems):
    width = into.shape[1]
    cols = pl.ds(pl.multiple_of(block * width, width), width)
    return [pltpu.make_async_copy(down_hbm.at[:, cols], into, sems.at[0])]


def gate_up_kernel(features, first, last, ahead, mine, other, *refs):
    refs = list(refs)
    if first:
        w_now, now_sems = refs.pop(), refs.pop()
    else:
        w_now, gate_in, up_in, squares_in = (refs.pop(0) for _ in range(4))
    if last:
        down_hbm, hidden_ref, next_w, both, sems = refs
        copies = down_fetch(chip_of(ahead), down_hbm, next_w, sems)
    else:
        gate_hbm, up_hbm, gate_out, up_out, squares_out, *mark, next_w, both, sems = refs
        copies = gate_up_fetch(chip_of(ahead), gate_hbm, up_hbm, next_w, sems)
    if first:

        def fetch_piece(n):
            cols = pl.ds(pl.multiple_of(n * COLS, COLS), COLS)
            return gate_up_fetch(chip_of(0), gate_hbm, up_hbm, w_now, now_sems.at[n], cols)

        for n in range(w_now.shape[2] // COLS):
            fetch(fetch_piece(n))
    fetch(copies)
    width = mine.shape[1]
    tokens = both.shape[0]
    core = lax.axis_index(AXIS) % 2
    squares = 0.0 if first else squares_in[...]
    for which, ref in enumerate((mine, other)):
        start = pl.multiple_of((core ^ which) * width, width)
        both[:, pl.ds(start, width)] = ref[:tokens]
        parts = ref[tokens:].astype(jnp.float32)[: EXTRA // 2]
        squares = squares + jnp.sum(parts[:, :tokens], axis=0, keepdims=True)
    if last:
        inv = lax.rsqrt(squares / features + EPS)
        inv = jnp.transpose(jnp.broadcast_to(inv, (8, tokens)))[:, :1]
    else:
        squares_out[...] = squares
        for ref in mark:
            ref[...] = jnp.zeros_like(ref)
    units = hidden_ref.shape[1] if last else gate_out.shape[1]
    def block(n, _):
        cols = pl.ds(pl.multiple_of(n * COLS, COLS), COLS)
        if first:
            for copy in fetch_piece(n):
                copy.wait()
        gate = jnp.dot(both[...], w_now[0, :, cols], preferred_element_type=jnp.float32)
        up = jnp.dot(both[...], w_now[1, :, cols], preferred_element_type=jnp.float32)
        if not first:
            gate = gate_in[:, cols] + gate
            up = up_in[:, cols] + up
        if last:
            gate = gate * inv
            value = gate / (1.0 + jnp.exp(-gate)) * (up * inv)
            hidden_ref[:, cols] = value.astype(jnp.bfloat16)
        else:
            gate_out[:, cols] = gate
            up_out[:, cols] = up
        return 0

    lax.fori_loop(0, units // COLS, block, 0)
    landed(copies)


def vmem():
    return pl.BlockSpec(memory_space=pltpu.VMEM)


def smem():
    return pl.BlockSpec(memory_space=pltpu.SMEM)


def anywhere():
    return pl.BlockSpec(memory_space=pl.ANY)


def in_hbm():
    return pl.BlockSpec(memory_space=pltpu.HBM)


def in_vmem(value):
    return pltpu.with_memory_space_constraint(value, pltpu.VMEM)


def params():
    return pltpu.CompilerParams(vmem_limit_bytes=VMEM_LIMIT)


def gate_up(ahead, mine, other, w_now, sums, weights, features, marked, last, next_shape, share):
    tokens, width = mine.shape[0] - EXTRA, mine.shape[1]
    units = weights[0].shape[1 - last]
    first = sums is None
    acc = pltpu.VMEM((tokens, units), jnp.float32)
    if last:
        out_shape = [pltpu.VMEM((tokens, units), jnp.bfloat16)]
    else:
        out_shape = [acc, acc, jax.ShapeDtypeStruct((1, tokens), jnp.float32)]
        if marked:
            out_shape.append(jax.ShapeDtypeStruct((EXTRA // 2, width), jnp.bfloat16))
    out_shape.append(pltpu.VMEM(next_shape, jnp.bfloat16))
    scratch = [pltpu.VMEM((tokens, 2 * width), jnp.bfloat16), pltpu.SemaphoreType.DMA((2,))]
    if first:
        scratch.append(pltpu.SemaphoreType.DMA((-(-units // COLS), 2)))
        scratch.append(pltpu.VMEM(next_shape, jnp.bfloat16))
    operands = [mine, other]
    in_specs = [vmem(), vmem()]
    aliases = {}
    if not first:
        operands.append(in_vmem(w_now))
        in_specs.append(vmem())
        if not last:
            aliases = {3: 0, 4: 1, 5: 2}
        operands += [in_vmem(total) for total in sums[:2]] + [sums[2]]
        in_specs += [vmem(), vmem(), vmem()]
    operands += list(weights)
    in_specs += [in_hbm() for _ in weights]
    return pl.pallas_call(
        functools.partial(gate_up_kernel, features, first, last, ahead),
        in_specs=in_specs,
        out_specs=[vmem() for _ in out_shape],
        out_shape=out_shape,
        scratch_shapes=scratch,
        input_output_aliases=aliases,
        compiler_params=params(),
        cost_estimate=cost(8 * tokens * width * units, 8 * width * units, share),
        name="gate_up",
    )(*operands)


def down_kernel(last, deps, ahead, hidden_ref, w_now, *refs):
    refs = list(refs[deps:])
    if not last:
        down_hbm, send_ref, keep_ref, next_w, sems = refs
        copies = down_fetch(chip_of(ahead), down_hbm, next_w, sems)
        fetch(copies)
    else:
        send_ref, keep_ref = refs
    width = send_ref.shape[1]
    core = lax.axis_index(AXIS) % 2
    def block(n, _):
        for which, out in ((1, send_ref), (0, keep_ref)):
            start = pl.multiple_of((core ^ which) * width + n * COLS, COLS)
            product = jnp.dot(
                hidden_ref[...], w_now[:, pl.ds(start, COLS)], preferred_element_type=jnp.float32
            )
            out[:, pl.ds(pl.multiple_of(n * COLS, COLS), COLS)] = product.astype(out.dtype)
        return 0

    lax.fori_loop(0, width // COLS, block, 0)
    if not last:
        landed(copies)


def down(ahead, hidden, w_now, down_weight, width, after):
    tokens, units = hidden.shape
    last = down_weight is None
    out_shape = [
        jax.ShapeDtypeStruct((tokens, width), jnp.bfloat16),
        jax.ShapeDtypeStruct((tokens, width), jnp.float32),
    ]
    operands = [in_vmem(hidden), in_vmem(w_now), *after]
    in_specs = [vmem(), vmem()] + [anywhere() for _ in after]
    scratch = []
    if not last:
        operands.append(down_weight)
        in_specs.append(in_hbm())
        out_shape.append(pltpu.VMEM(w_now.shape, jnp.bfloat16))
        scratch = [pltpu.SemaphoreType.DMA((1,))]
    return pl.pallas_call(
        functools.partial(down_kernel, last, len(after), ahead),
        in_specs=in_specs,
        out_specs=[vmem() for _ in out_shape],
        out_shape=out_shape,
        scratch_shapes=scratch,
        compiler_params=params(),
        cost_estimate=cost(4 * tokens * units * width, 4 * units * width, DOWN_SHARE),
        name="down",
    )(*operands)


def held(chunk, after):
    return lax.dynamic_update_slice(chunk, after, (chunk.shape[0] - after.shape[0], 0))


CORE, X, Z1, Z2, Z3 = 1, 2, 4, 8, 12


def per_device(activations, norm_gain, gate_weight, up_weight, down_weight):
    tokens, width = activations.shape
    features, units = gate_weight.shape

    order = [0, X, Z1, Z1 | X, Z3, Z3 | X, Z2, Z2 | X]
    there, here = X, 0
    blocks = [
        Z2 | there, Z1 | there, Z3 | there, Z2 | here, 0 | there, Z3 | here, Z1 | here, 0 | here
    ]

    gate_weight, up_weight, down_weight = (
        pltpu.with_memory_space_constraint(w, pltpu.HBM)
        for w in (gate_weight, up_weight, down_weight)
    )
    w_now = None
    rows = activations.astype(jnp.float32)
    scaled = (rows * norm_gain.astype(jnp.float32)[None, :]).astype(jnp.bfloat16)
    left = jnp.pad(jnp.sum(rows * rows, axis=1), (0, width - tokens))
    parts = []
    for _ in range(3):
        parts.append(lax.reduce_precision(left, 8, 7))
        left = left - parts[-1]
    extra = jnp.pad(jnp.stack(parts), ((0, EXTRA - 3), (0, 0))).astype(jnp.bfloat16)
    own = jnp.concatenate([scaled, extra])

    raw = {0: own, X: swap(own, X), Z3: swap(own, Z3), Z1: swap(own, Z1)}
    sums = None
    for n, mask in enumerate(order):
        last = n == len(order) - 1
        *sums, w_now = gate_up(
            blocks[0] if last else order[n + 1],
            raw[mask],
            swap(raw[mask], CORE),
            w_now,
            sums,
            (down_weight,) if last else (gate_weight, up_weight),
            features,
            n < 2,
            last,
            (units, 2 * width) if last else (2, 2 * width, units),
            GATE_UP_SHARE[n],
        )
        if n < 2:
            mark = sums.pop()
        if n == 0:
            raw[Z1] = held(raw[Z1], mark)
            raw[Z1 | X] = swap(raw[Z1], X)
        if n == 1:
            raw[Z3] = held(raw[Z3], mark)
            raw[Z2] = swap(raw[Z3], Z1)
            raw[Z3 | X] = swap(raw[Z3], X)
            raw[Z2 | X] = swap(raw[Z2], X)
    hidden = sums[0]

    def down_block(n, after):
        last = n == len(blocks) - 1
        send, keep, *w_next = down(
            0 if last else blocks[n + 1], hidden, w_now, None if last else down_weight,
            width, after,
        )
        return w_next[0] if w_next else None, keep + wide(swap(send, CORE))

    w_now, pair = down_block(0, [])
    over_far = narrow(pair)
    w_now, pair = down_block(1, [])
    turn = narrow(pair)
    w_now, pair = down_block(2, [over_far])
    over_next = narrow(pair)
    w_now, far = down_block(3, [turn])
    far = far + wide(swap(over_far, X))
    w_now, pair = down_block(4, [over_next])
    over_here = narrow(pair + wide(swap(turn, Z1)))
    far = narrow(far)
    w_now, next_far = down_block(5, [far])
    next_far = next_far + wide(swap(over_next, X))
    w_now, near = down_block(6, [over_here])
    next_far = narrow(next_far + wide(swap(far, Z1)))
    _, total = down_block(7, [next_far])
    total = total + wide(swap(narrow(near), Z1)) + wide(swap(over_here, X))
    return narrow(total + wide(swap(next_far, Z3)))


def wide(value):
    return value.astype(jnp.float32)


def narrow(value):
    return value.astype(jnp.bfloat16)


def fits(activations):
    tokens, width = activations.shape
    return tokens % 16 == 0 and tokens <= width


def solution(mesh):
    in_specs = (P("groups", AXIS), P(AXIS), P(None, AXIS), P(None, AXIS), P(AXIS, None))
    out_specs = P("groups", AXIS)

    def body(activations, norm_gain, gate_weight, up_weight, down_weight):
        if mesh.shape[AXIS] == 16 and activations.shape[1] % 128 == 0 and fits(activations):
            run = per_device
        else:
            run = functools.partial(plain_per_device, gate_weight.shape[0])
        return run(activations, norm_gain, gate_weight, up_weight, down_weight)

    return jax.shard_map(
        body, mesh=mesh, in_specs=in_specs, out_specs=out_specs, check_vma=False
    )
```

```python
import functools

import jax
import jax.numpy as jnp
from jax import lax
from jax.experimental import pallas as pl
from jax.experimental.pallas import tpu as pltpu
from jax.sharding import PartitionSpec as P

EPS = 1e-05
AXIS = "row"
VMEM_LIMIT = 16 * 1024 * 1024


def plain_per_device(features, activations, norm_gain, gate_weight, up_weight, down_weight):
    float_rows = activations.astype(jnp.float32)
    square_sums = lax.psum(jnp.sum(float_rows * float_rows, axis=1), AXIS)
    inv_scale = lax.rsqrt(square_sums / features + EPS)
    normed = (float_rows * inv_scale[:, None] * norm_gain.astype(jnp.float32)[None, :]).astype(
        jnp.bfloat16
    )
    shard_rows = lax.all_gather(normed, AXIS, axis=1, tiled=True)
    gate_proj = jnp.dot(shard_rows, gate_weight, preferred_element_type=jnp.float32)
    up_proj = jnp.dot(shard_rows, up_weight, preferred_element_type=jnp.float32)
    hidden = (jax.nn.silu(gate_proj) * up_proj).astype(jnp.bfloat16)
    reduced = lax.psum_scatter(
        lax.dot_general(
            down_weight, hidden, (((0,), (1,)), ((), ())), preferred_element_type=jnp.float32
        ),
        AXIS,
        scatter_dimension=0,
        tiled=True,
    )
    return reduced.T.astype(jnp.bfloat16)


def swap(value, mask):
    return lax.ppermute(value, AXIS, [(i, i ^ mask) for i in range(lax.axis_size(AXIS))])


COLS = 256
EXTRA = 16
FIRST_SHARE, GATE_UP_SHARE, DOWN_SHARE = 4, (2, 2, 2, 2, 2, 2, 2, 2), 3


def cost(flops, weight_bytes, share):
    return pl.CostEstimate(
        flops=int(flops * share), bytes_accessed=int(weight_bytes * share), transcendentals=0
    )


def fetch(copies):
    for copy in copies:
        copy.start()


def landed(copies):
    for copy in copies:
        copy.wait()


def chip_of(mask):
    return lax.axis_index(AXIS) // 2 ^ mask // 2


def gate_up_fetch(block, gate_hbm, up_hbm, into, sems, cols=slice(None)):
    depth = into.shape[1]
    rows = pl.ds(pl.multiple_of(block * depth, depth), depth)
    return [
        pltpu.make_async_copy(hbm.at[rows, cols], into.at[n, :, cols], sems.at[n])
        for n, hbm in enumerate((gate_hbm, up_hbm))
    ]


def down_fetch(block, down_hbm, into, sems):
    width = into.shape[1]
    cols = pl.ds(pl.multiple_of(block * width, width), width)
    return [pltpu.make_async_copy(down_hbm.at[:, cols], into, sems.at[0])]


def first_fetch_kernel(gate_hbm, up_hbm, mark, next_w, sems):
    copies = gate_up_fetch(chip_of(0), gate_hbm, up_hbm, next_w, sems)
    fetch(copies)
    mark[...] = jnp.zeros_like(mark)
    landed(copies)


def gate_up_kernel(features, first, last, ahead, mine, other, *refs):
    refs = list(refs)
    w_now = refs.pop(0)
    if not first:
        gate_in, up_in, squares_in = refs.pop(0), refs.pop(0), refs.pop(0)
    if last:
        down_hbm, hidden_ref, next_w, both, sems = refs
        copies = down_fetch(chip_of(ahead), down_hbm, next_w, sems)
    else:
        gate_hbm, up_hbm, gate_out, up_out, squares_out, *mark, next_w, both, sems = refs
        copies = gate_up_fetch(chip_of(ahead), gate_hbm, up_hbm, next_w, sems)
    fetch(copies)
    width = mine.shape[1]
    tokens = both.shape[0]
    core = lax.axis_index(AXIS) % 2
    squares = 0.0 if first else squares_in[...]
    for which, ref in enumerate((mine, other)):
        start = pl.multiple_of((core ^ which) * width, width)
        both[:, pl.ds(start, width)] = ref[:tokens]
        parts = ref[tokens:].astype(jnp.float32)[: EXTRA // 2]
        squares = squares + jnp.sum(parts[:, :tokens], axis=0, keepdims=True)
    if last:
        inv = lax.rsqrt(squares / features + EPS)
        inv = jnp.transpose(jnp.broadcast_to(inv, (8, tokens)))[:, :1]
    else:
        squares_out[...] = squares
        for ref in mark:
            ref[...] = jnp.zeros_like(ref)
    units = hidden_ref.shape[1] if last else gate_out.shape[1]
    def block(n, _):
        cols = pl.ds(pl.multiple_of(n * COLS, COLS), COLS)
        gate = jnp.dot(both[...], w_now[0, :, cols], preferred_element_type=jnp.float32)
        up = jnp.dot(both[...], w_now[1, :, cols], preferred_element_type=jnp.float32)
        if not first:
            gate = gate_in[:, cols] + gate
            up = up_in[:, cols] + up
        if last:
            gate = gate * inv
            value = gate / (1.0 + jnp.exp(-gate)) * (up * inv)
            hidden_ref[:, cols] = value.astype(jnp.bfloat16)
        else:
            gate_out[:, cols] = gate
            up_out[:, cols] = up
        return 0

    lax.fori_loop(0, units // COLS, block, 0)
    landed(copies)


def vmem():
    return pl.BlockSpec(memory_space=pltpu.VMEM)


def smem():
    return pl.BlockSpec(memory_space=pltpu.SMEM)


def anywhere():
    return pl.BlockSpec(memory_space=pl.ANY)


def in_hbm():
    return pl.BlockSpec(memory_space=pltpu.HBM)


def in_vmem(value):
    return pltpu.with_memory_space_constraint(value, pltpu.VMEM)


def params():
    return pltpu.CompilerParams(vmem_limit_bytes=VMEM_LIMIT)


def first_fetch(gate_weight, up_weight, width):
    units = gate_weight.shape[1]
    return pl.pallas_call(
        first_fetch_kernel,
        in_specs=[in_hbm(), in_hbm()],
        out_specs=[vmem(), vmem()],
        out_shape=[
            jax.ShapeDtypeStruct((EXTRA // 2, width), jnp.bfloat16),
            pltpu.VMEM((2, 2 * width, units), jnp.bfloat16),
        ],
        scratch_shapes=[pltpu.SemaphoreType.DMA((2,))],
        compiler_params=params(),
        cost_estimate=cost(0, 8 * width * units, FIRST_SHARE),
        name="first_fetch",
    )(gate_weight, up_weight)


def gate_up(ahead, mine, other, w_now, sums, weights, features, marked, last, next_shape, share):
    tokens, width = mine.shape[0] - EXTRA, mine.shape[1]
    units = weights[0].shape[1 - last]
    first = sums is None
    acc = pltpu.VMEM((tokens, units), jnp.float32)
    if last:
        out_shape = [pltpu.VMEM((tokens, units), jnp.bfloat16)]
    else:
        out_shape = [acc, acc, jax.ShapeDtypeStruct((1, tokens), jnp.float32)]
        if marked:
            out_shape.append(jax.ShapeDtypeStruct((EXTRA // 2, width), jnp.bfloat16))
    out_shape.append(pltpu.VMEM(next_shape, jnp.bfloat16))
    scratch = [pltpu.VMEM((tokens, 2 * width), jnp.bfloat16), pltpu.SemaphoreType.DMA((2,))]
    operands = [mine, other, in_vmem(w_now)]
    in_specs = [vmem(), vmem(), vmem()]
    aliases = {}
    if not first:
        if not last:
            aliases = {3: 0, 4: 1, 5: 2}
        operands += [in_vmem(total) for total in sums[:2]] + [sums[2]]
        in_specs += [vmem(), vmem(), vmem()]
    operands += list(weights)
    in_specs += [in_hbm() for _ in weights]
    return pl.pallas_call(
        functools.partial(gate_up_kernel, features, first, last, ahead),
        in_specs=in_specs,
        out_specs=[vmem() for _ in out_shape],
        out_shape=out_shape,
        scratch_shapes=scratch,
        input_output_aliases=aliases,
        compiler_params=params(),
        cost_estimate=cost(8 * tokens * width * units, 8 * width * units, share),
        name="gate_up",
    )(*operands)


def down_kernel(last, deps, ahead, hidden_ref, w_now, *refs):
    refs = list(refs[deps:])
    if not last:
        down_hbm, send_ref, keep_ref, next_w, sems = refs
        copies = down_fetch(chip_of(ahead), down_hbm, next_w, sems)
        fetch(copies)
    else:
        send_ref, keep_ref = refs
    width = send_ref.shape[1]
    core = lax.axis_index(AXIS) % 2
    def block(n, _):
        for which, out in ((1, send_ref), (0, keep_ref)):
            start = pl.multiple_of((core ^ which) * width + n * COLS, COLS)
            product = jnp.dot(
                hidden_ref[...], w_now[:, pl.ds(start, COLS)], preferred_element_type=jnp.float32
            )
            out[:, pl.ds(pl.multiple_of(n * COLS, COLS), COLS)] = product.astype(out.dtype)
        return 0

    lax.fori_loop(0, width // COLS, block, 0)
    if not last:
        landed(copies)


def down(ahead, hidden, w_now, down_weight, width, after):
    tokens, units = hidden.shape
    last = down_weight is None
    out_shape = [
        jax.ShapeDtypeStruct((tokens, width), jnp.bfloat16),
        jax.ShapeDtypeStruct((tokens, width), jnp.float32),
    ]
    operands = [in_vmem(hidden), in_vmem(w_now), *after]
    in_specs = [vmem(), vmem()] + [anywhere() for _ in after]
    scratch = []
    if not last:
        operands.append(down_weight)
        in_specs.append(in_hbm())
        out_shape.append(pltpu.VMEM(w_now.shape, jnp.bfloat16))
        scratch = [pltpu.SemaphoreType.DMA((1,))]
    return pl.pallas_call(
        functools.partial(down_kernel, last, len(after), ahead),
        in_specs=in_specs,
        out_specs=[vmem() for _ in out_shape],
        out_shape=out_shape,
        scratch_shapes=scratch,
        compiler_params=params(),
        cost_estimate=cost(4 * tokens * units * width, 4 * units * width, DOWN_SHARE),
        name="down",
    )(*operands)


def held(chunk, after):
    return lax.dynamic_update_slice(chunk, after, (chunk.shape[0] - after.shape[0], 0))


CORE, X, Z1, Z2, Z3 = 1, 2, 4, 8, 12


def per_device(activations, norm_gain, gate_weight, up_weight, down_weight):
    tokens, width = activations.shape
    features, units = gate_weight.shape

    order = [0, X, Z1, Z1 | X, Z3, Z3 | X, Z2, Z2 | X]
    there, here = X, 0
    blocks = [
        Z2 | there, Z1 | there, Z3 | there, Z2 | here, 0 | there, Z3 | here, Z1 | here, 0 | here
    ]

    gate_weight, up_weight, down_weight = (
        pltpu.with_memory_space_constraint(w, pltpu.HBM)
        for w in (gate_weight, up_weight, down_weight)
    )
    mark, w_now = first_fetch(gate_weight, up_weight, width)
    rows = activations.astype(jnp.float32)
    scaled = (rows * norm_gain.astype(jnp.float32)[None, :]).astype(jnp.bfloat16)
    left = jnp.pad(jnp.sum(rows * rows, axis=1), (0, width - tokens))
    parts = []
    for _ in range(3):
        parts.append(lax.reduce_precision(left, 8, 7))
        left = left - parts[-1]
    extra = jnp.pad(jnp.stack(parts), ((0, EXTRA - 3), (0, 0))).astype(jnp.bfloat16)
    own = jnp.concatenate([scaled, extra])

    raw = {0: own, X: swap(own, X), Z3: swap(own, Z3), Z1: swap(own, Z1)}
    sums, marked = None, (0, 1, 3, 5)
    for n, mask in enumerate(order):
        last = n == len(order) - 1
        *sums, w_now = gate_up(
            blocks[0] if last else order[n + 1],
            raw[mask],
            swap(raw[mask], CORE),
            w_now,
            sums,
            (down_weight,) if last else (gate_weight, up_weight),
            features,
            n in marked,
            last,
            (units, 2 * width) if last else (2, 2 * width, units),
            GATE_UP_SHARE[n],
        )
        if n in marked:
            mark = sums.pop()
        if n == 0:
            raw[Z1] = held(raw[Z1], mark)
            raw[Z1 | X] = swap(raw[Z1], X)
        if n == 1:
            raw[Z3] = held(raw[Z3], mark)
            raw[Z2] = swap(raw[Z3], Z1)
            raw[Z3 | X] = swap(raw[Z3], X)
        if n == 3:
            raw[Z2] = held(raw[Z2], mark)
            raw[Z2 | X] = swap(raw[Z2], X)
        if n == 5:
            raw[Z2 | X] = held(raw[Z2 | X], mark)
    hidden = sums[0]

    def down_block(n, after):
        last = n == len(blocks) - 1
        send, keep, *w_next = down(
            0 if last else blocks[n + 1], hidden, w_now, None if last else down_weight,
            width, after,
        )
        return w_next[0] if w_next else None, keep + wide(swap(send, CORE))

    w_now, pair = down_block(0, [])
    over_far = narrow(pair)
    w_now, pair = down_block(1, [])
    turn = narrow(pair)
    w_now, pair = down_block(2, [over_far])
    over_next = narrow(pair)
    w_now, far = down_block(3, [turn])
    far = far + wide(swap(over_far, X))
    w_now, pair = down_block(4, [over_next])
    over_here = narrow(pair + wide(swap(turn, Z1)))
    far = narrow(far)
    w_now, next_far = down_block(5, [far])
    next_far = next_far + wide(swap(over_next, X))
    w_now, near = down_block(6, [over_here])
    next_far = narrow(next_far + wide(swap(far, Z1)))
    _, total = down_block(7, [next_far])
    total = total + wide(swap(narrow(near), Z1)) + wide(swap(over_here, X))
    return narrow(total + wide(swap(next_far, Z3)))


def wide(value):
    return value.astype(jnp.float32)


def narrow(value):
    return value.astype(jnp.bfloat16)


def fits(activations):
    tokens, width = activations.shape
    return tokens % 16 == 0 and tokens <= width


def solution(mesh):
    in_specs = (P("groups", AXIS), P(AXIS), P(None, AXIS), P(None, AXIS), P(AXIS, None))
    out_specs = P("groups", AXIS)

    def body(activations, norm_gain, gate_weight, up_weight, down_weight):
        if mesh.shape[AXIS] == 16 and activations.shape[1] % 128 == 0 and fits(activations):
            run = per_device
        else:
            run = functools.partial(plain_per_device, gate_weight.shape[0])
        return run(activations, norm_gain, gate_weight, up_weight, down_weight)

    return jax.shard_map(
        body, mesh=mesh, in_specs=in_specs, out_specs=out_specs, check_vma=False
    )
```

```python
import functools

import jax
import jax.numpy as jnp
from jax import lax
from jax.experimental import pallas as pl
from jax.experimental.pallas import tpu as pltpu
from jax.sharding import PartitionSpec as P

EPS = 1e-05
AXIS = "row"
VMEM_LIMIT = 16 * 1024 * 1024


def plain_per_device(features, activations, norm_gain, gate_weight, up_weight, down_weight):
    float_rows = activations.astype(jnp.float32)
    square_sums = lax.psum(jnp.sum(float_rows * float_rows, axis=1), AXIS)
    inv_scale = lax.rsqrt(square_sums / features + EPS)
    normed = (float_rows * inv_scale[:, None] * norm_gain.astype(jnp.float32)[None, :]).astype(
        jnp.bfloat16
    )
    shard_rows = lax.all_gather(normed, AXIS, axis=1, tiled=True)
    gate_proj = jnp.dot(shard_rows, gate_weight, preferred_element_type=jnp.float32)
    up_proj = jnp.dot(shard_rows, up_weight, preferred_element_type=jnp.float32)
    hidden = (jax.nn.silu(gate_proj) * up_proj).astype(jnp.bfloat16)
    reduced = lax.psum_scatter(
        lax.dot_general(
            down_weight, hidden, (((0,), (1,)), ((), ())), preferred_element_type=jnp.float32
        ),
        AXIS,
        scatter_dimension=0,
        tiled=True,
    )
    return reduced.T.astype(jnp.bfloat16)


def swap(value, mask):
    return lax.ppermute(value, AXIS, [(i, i ^ mask) for i in range(lax.axis_size(AXIS))])


COLS = 256
EXTRA = 16
FIRST_SHARE, GATE_UP_SHARE, DOWN_SHARE = 4, (2, 2, 2, 2, 2, 2, 2, 2), 3


def cost(flops, weight_bytes, share):
    return pl.CostEstimate(
        flops=int(flops * share), bytes_accessed=int(weight_bytes * share), transcendentals=0
    )


def fetch(copies):
    for copy in copies:
        copy.start()


def landed(copies):
    for copy in copies:
        copy.wait()


def chip_of(mask):
    return lax.axis_index(AXIS) // 2 ^ mask // 2


def gate_up_fetch(block, gate_hbm, up_hbm, into, sems, cols=slice(None)):
    depth = into.shape[1]
    rows = pl.ds(pl.multiple_of(block * depth, depth), depth)
    return [
        pltpu.make_async_copy(hbm.at[rows, cols], into.at[n, :, cols], sems.at[n])
        for n, hbm in enumerate((gate_hbm, up_hbm))
    ]


def down_fetch(block, down_hbm, into, sems):
    width = into.shape[1]
    cols = pl.ds(pl.multiple_of(block * width, width), width)
    return [pltpu.make_async_copy(down_hbm.at[:, cols], into, sems.at[0])]


def first_fetch_kernel(gate_hbm, up_hbm, mark, next_w, sems):
    copies = gate_up_fetch(chip_of(0), gate_hbm, up_hbm, next_w, sems)
    fetch(copies)
    mark[...] = jnp.zeros_like(mark)
    landed(copies)


def gate_up_kernel(features, first, last, ahead, mine, other, *refs):
    refs = list(refs)
    w_now = refs.pop(0)
    if not first:
        gate_in, up_in, squares_in = refs.pop(0), refs.pop(0), refs.pop(0)
    if last:
        down_hbm, hidden_ref, next_w, both, sems = refs
        copies = down_fetch(chip_of(ahead), down_hbm, next_w, sems)
    else:
        gate_hbm, up_hbm, gate_out, up_out, squares_out, *mark, next_w, both, sems = refs
        copies = gate_up_fetch(chip_of(ahead), gate_hbm, up_hbm, next_w, sems)
    fetch(copies)
    width = mine.shape[1]
    tokens = both.shape[0]
    core = lax.axis_index(AXIS) % 2
    squares = 0.0 if first else squares_in[...]
    for which, ref in enumerate((mine, other)):
        start = pl.multiple_of((core ^ which) * width, width)
        both[:, pl.ds(start, width)] = ref[:tokens]
        parts = ref[tokens:].astype(jnp.float32)[: EXTRA // 2]
        squares = squares + jnp.sum(parts[:, :tokens], axis=0, keepdims=True)
    if last:
        inv = lax.rsqrt(squares / features + EPS)
        inv = jnp.transpose(jnp.broadcast_to(inv, (8, tokens)))[:, :1]
    else:
        squares_out[...] = squares
        for ref in mark:
            ref[...] = jnp.zeros_like(ref)
    units = hidden_ref.shape[1] if last else gate_out.shape[1]
    def block(n, _):
        cols = pl.ds(n * COLS if isinstance(n, int) else pl.multiple_of(n * COLS, COLS), COLS)
        gate = jnp.dot(both[...], w_now[0, :, cols], preferred_element_type=jnp.float32)
        up = jnp.dot(both[...], w_now[1, :, cols], preferred_element_type=jnp.float32)
        if not first:
            gate = gate_in[:, cols] + gate
            up = up_in[:, cols] + up
        if last:
            gate = gate * inv
            value = gate / (1.0 + jnp.exp(-gate)) * (up * inv)
            hidden_ref[:, cols] = value.astype(jnp.bfloat16)
        else:
            gate_out[:, cols] = gate
            up_out[:, cols] = up
        return 0

    def two_blocks(n, _):
        return block(2 * n + 1, block(2 * n, 0))

    blocks = units // COLS
    lax.fori_loop(0, blocks // 2, two_blocks, 0)
    if blocks % 2:
        block(blocks - 1, 0)
    landed(copies)


def vmem():
    return pl.BlockSpec(memory_space=pltpu.VMEM)


def smem():
    return pl.BlockSpec(memory_space=pltpu.SMEM)


def anywhere():
    return pl.BlockSpec(memory_space=pl.ANY)


def in_hbm():
    return pl.BlockSpec(memory_space=pltpu.HBM)


def in_vmem(value):
    return pltpu.with_memory_space_constraint(value, pltpu.VMEM)


def params():
    return pltpu.CompilerParams(vmem_limit_bytes=VMEM_LIMIT)


def first_fetch(gate_weight, up_weight, width):
    units = gate_weight.shape[1]
    return pl.pallas_call(
        first_fetch_kernel,
        in_specs=[in_hbm(), in_hbm()],
        out_specs=[vmem(), vmem()],
        out_shape=[
            jax.ShapeDtypeStruct((EXTRA // 2, width), jnp.bfloat16),
            pltpu.VMEM((2, 2 * width, units), jnp.bfloat16),
        ],
        scratch_shapes=[pltpu.SemaphoreType.DMA((2,))],
        compiler_params=params(),
        cost_estimate=cost(0, 8 * width * units, FIRST_SHARE),
        name="first_fetch",
    )(gate_weight, up_weight)


def gate_up(ahead, mine, other, w_now, sums, weights, features, marked, last, next_shape, share):
    tokens, width = mine.shape[0] - EXTRA, mine.shape[1]
    units = weights[0].shape[1 - last]
    first = sums is None
    acc = pltpu.VMEM((tokens, units), jnp.float32)
    if last:
        out_shape = [pltpu.VMEM((tokens, units), jnp.bfloat16)]
    else:
        out_shape = [acc, acc, jax.ShapeDtypeStruct((1, tokens), jnp.float32)]
        if marked:
            out_shape.append(jax.ShapeDtypeStruct((EXTRA // 2, width), jnp.bfloat16))
    out_shape.append(pltpu.VMEM(next_shape, jnp.bfloat16))
    scratch = [pltpu.VMEM((tokens, 2 * width), jnp.bfloat16), pltpu.SemaphoreType.DMA((2,))]
    operands = [mine, other, in_vmem(w_now)]
    in_specs = [vmem(), vmem(), vmem()]
    aliases = {}
    if not first:
        if not last:
            aliases = {3: 0, 4: 1, 5: 2}
        operands += [in_vmem(total) for total in sums[:2]] + [sums[2]]
        in_specs += [vmem(), vmem(), vmem()]
    operands += list(weights)
    in_specs += [in_hbm() for _ in weights]
    return pl.pallas_call(
        functools.partial(gate_up_kernel, features, first, last, ahead),
        in_specs=in_specs,
        out_specs=[vmem() for _ in out_shape],
        out_shape=out_shape,
        scratch_shapes=scratch,
        input_output_aliases=aliases,
        compiler_params=params(),
        cost_estimate=cost(8 * tokens * width * units, 8 * width * units, share),
        name="gate_up",
    )(*operands)


def down_kernel(last, deps, ahead, hidden_ref, w_now, *refs):
    refs = list(refs[deps:])
    if not last:
        down_hbm, send_ref, keep_ref, next_w, sems = refs
        copies = down_fetch(chip_of(ahead), down_hbm, next_w, sems)
        fetch(copies)
    else:
        send_ref, keep_ref = refs
    width = send_ref.shape[1]
    core = lax.axis_index(AXIS) % 2
    def block(n, _):
        for which, out in ((1, send_ref), (0, keep_ref)):
            start = pl.multiple_of((core ^ which) * width + n * COLS, COLS)
            product = jnp.dot(
                hidden_ref[...], w_now[:, pl.ds(start, COLS)], preferred_element_type=jnp.float32
            )
            out[:, pl.ds(pl.multiple_of(n * COLS, COLS), COLS)] = product.astype(out.dtype)
        return 0

    lax.fori_loop(0, width // COLS, block, 0)
    if not last:
        landed(copies)


def down(ahead, hidden, w_now, down_weight, width, after):
    tokens, units = hidden.shape
    last = down_weight is None
    out_shape = [
        jax.ShapeDtypeStruct((tokens, width), jnp.bfloat16),
        jax.ShapeDtypeStruct((tokens, width), jnp.float32),
    ]
    operands = [in_vmem(hidden), in_vmem(w_now), *after]
    in_specs = [vmem(), vmem()] + [anywhere() for _ in after]
    scratch = []
    if not last:
        operands.append(down_weight)
        in_specs.append(in_hbm())
        out_shape.append(pltpu.VMEM(w_now.shape, jnp.bfloat16))
        scratch = [pltpu.SemaphoreType.DMA((1,))]
    return pl.pallas_call(
        functools.partial(down_kernel, last, len(after), ahead),
        in_specs=in_specs,
        out_specs=[vmem() for _ in out_shape],
        out_shape=out_shape,
        scratch_shapes=scratch,
        compiler_params=params(),
        cost_estimate=cost(4 * tokens * units * width, 4 * units * width, DOWN_SHARE),
        name="down",
    )(*operands)


def held(chunk, after):
    return lax.dynamic_update_slice(chunk, after, (chunk.shape[0] - after.shape[0], 0))


CORE, X, Z1, Z2, Z3 = 1, 2, 4, 8, 12


def per_device(activations, norm_gain, gate_weight, up_weight, down_weight):
    tokens, width = activations.shape
    features, units = gate_weight.shape

    order = [0, X, Z1, Z1 | X, Z3, Z3 | X, Z2, Z2 | X]
    there, here = X, 0
    blocks = [
        Z2 | there, Z1 | there, Z3 | there, Z2 | here, 0 | there, Z3 | here, Z1 | here, 0 | here
    ]

    gate_weight, up_weight, down_weight = (
        pltpu.with_memory_space_constraint(w, pltpu.HBM)
        for w in (gate_weight, up_weight, down_weight)
    )
    mark, w_now = first_fetch(gate_weight, up_weight, width)
    rows = activations.astype(jnp.float32)
    scaled = (rows * norm_gain.astype(jnp.float32)[None, :]).astype(jnp.bfloat16)
    left = jnp.pad(jnp.sum(rows * rows, axis=1), (0, width - tokens))
    parts = []
    for _ in range(3):
        parts.append(lax.reduce_precision(left, 8, 7))
        left = left - parts[-1]
    extra = jnp.pad(jnp.stack(parts), ((0, EXTRA - 3), (0, 0))).astype(jnp.bfloat16)
    own = jnp.concatenate([scaled, extra])

    raw = {0: own, X: swap(own, X), Z3: swap(own, Z3), Z1: swap(own, Z1)}
    sums, marked = None, (0, 1, 3, 5)
    for n, mask in enumerate(order):
        last = n == len(order) - 1
        *sums, w_now = gate_up(
            blocks[0] if last else order[n + 1],
            raw[mask],
            swap(raw[mask], CORE),
            w_now,
            sums,
            (down_weight,) if last else (gate_weight, up_weight),
            features,
            n in marked,
            last,
            (units, 2 * width) if last else (2, 2 * width, units),
            GATE_UP_SHARE[n],
        )
        if n in marked:
            mark = sums.pop()
        if n == 0:
            raw[Z1] = held(raw[Z1], mark)
            raw[Z1 | X] = swap(raw[Z1], X)
        if n == 1:
            raw[Z3] = held(raw[Z3], mark)
            raw[Z2] = swap(raw[Z3], Z1)
            raw[Z3 | X] = swap(raw[Z3], X)
        if n == 3:
            raw[Z2] = held(raw[Z2], mark)
            raw[Z2 | X] = swap(raw[Z2], X)
        if n == 5:
            raw[Z2 | X] = held(raw[Z2 | X], mark)
    hidden = sums[0]

    def down_block(n, after):
        last = n == len(blocks) - 1
        send, keep, *w_next = down(
            0 if last else blocks[n + 1], hidden, w_now, None if last else down_weight,
            width, after,
        )
        return w_next[0] if w_next else None, keep + wide(swap(send, CORE))

    w_now, pair = down_block(0, [])
    over_far = narrow(pair)
    w_now, pair = down_block(1, [])
    turn = narrow(pair)
    w_now, pair = down_block(2, [over_far])
    over_next = narrow(pair)
    w_now, far = down_block(3, [turn])
    far = far + wide(swap(over_far, X))
    w_now, pair = down_block(4, [over_next])
    over_here = narrow(pair + wide(swap(turn, Z1)))
    far = narrow(far)
    w_now, next_far = down_block(5, [far])
    next_far = next_far + wide(swap(over_next, X))
    w_now, near = down_block(6, [over_here])
    next_far = narrow(next_far + wide(swap(far, Z1)))
    _, total = down_block(7, [next_far])
    total = total + wide(swap(narrow(near), Z1)) + wide(swap(over_here, X))
    return narrow(total + wide(swap(next_far, Z3)))


def wide(value):
    return value.astype(jnp.float32)


def narrow(value):
    return value.astype(jnp.bfloat16)


def fits(activations):
    tokens, width = activations.shape
    return tokens % 16 == 0 and tokens <= width


def solution(mesh):
    in_specs = (P("groups", AXIS), P(AXIS), P(None, AXIS), P(None, AXIS), P(AXIS, None))
    out_specs = P("groups", AXIS)

    def body(activations, norm_gain, gate_weight, up_weight, down_weight):
        if mesh.shape[AXIS] == 16 and activations.shape[1] % 128 == 0 and fits(activations):
            run = per_device
        else:
            run = functools.partial(plain_per_device, gate_weight.shape[0])
        return run(activations, norm_gain, gate_weight, up_weight, down_weight)

    return jax.shard_map(
        body, mesh=mesh, in_specs=in_specs, out_specs=out_specs, check_vma=False
    )
```
